32 devices in a mesh: parts: 2 (over x), leaf: 16 (over z, y, core).
Axes of the slice: x: 2, y: 2, z: 4, core: 2. Of those that a mesh axis runs over, the one named last changes fastest.
Arguments:
- charges: bfloat16 [1024, 64, 128], P(('parts', 'leaf')), parts along dimension 0, may hold values from -6 to 6
- near_blocks: bfloat16 [1024, 8, 128, 128], P(('parts', 'leaf')), parts along dimension 0, may hold values from -0.1875 to 0.1875
- near_index: int32 [1024, 8], P(('parts', 'leaf')), parts along dimension 0, may hold values from 0 to 511, as said below
- near_count: int32 [1024], P(('parts', 'leaf')), parts along dimension 0, may hold values from 1 to 8
- leaf_basis: bfloat16 [1024, 64, 128], P(('parts', 'leaf')), parts along dimension 0, may hold values from -0.5 to 0.5
- leaf_coupling: bfloat16 [1024, 8, 64, 64], P(('parts', 'leaf')), parts along dimension 0, may hold values from -0.25 to 0.25
- far_index: int32 [1024, 8], P(('parts', 'leaf')), parts along dimension 0, may hold values from 0 to 511, as said below
- transfer: bfloat16 [1024, 64, 64], P(('parts', 'leaf')), parts along dimension 0, may hold values from -0.75 to 0.75
- cluster_coupling: bfloat16 [32, 16, 64, 64], P(('parts', 'leaf')), parts along dimension 0, may hold values from -0.03125 to 0.03125
- cluster_index: int32 [32, 16], P(('parts', 'leaf')), parts along dimension 0, may hold values from 0 to 15, as said below
Outputs:
- potential: bfloat16 [1024, 64, 128], P(('parts', 'leaf')), parts along dimension 0
The draws below stay inside these ranges and needn't reach their ends.
There are 2 independent parts, one for each index of `parts`. The reference program is written for one: setup_inputs(seed, part) draws one part's arguments, and reference() takes and returns one part's arrays. A program takes and returns all parts, laid end to end along the dimension named above; each array names one. Nothing has to cross between parts.
Inputs may be any that keep to these rules, and one draw needn't show every extreme that they name: `near_index`: every entry is within 32 leaves of its own leaf, counted cyclically; slot 0 is the leaf itself; slots at or past near_count hold some valid leaf. `far_index`: every entry is within 32 leaves of its own leaf, counted cyclically. `cluster_index`: every entry is within 7 clusters of its own cluster, counted cyclically; entry 0 lies exactly 7 below and entry 1 exactly 7 above.
All inputs are finite; a program needn't handle non-finite values.
Results may differ from the reference program's by a relative error of at most 0.0054.
Values may be sent and summed in bfloat16 or wider, within the bound.
A program may use at most 128 MiB of HBM per device.

```python
import jax
import jax.numpy as jnp
from jax import lax

LS = 128
RANK = 64
RHS = 64
LDEV = 32
NEAR = 8
FARL = 8
FARC = 16
LEAVES = 512
CLUSTERS = 16


def draw_near_index(key, part):
    key = jax.random.fold_in(key, 1)
    offsets = jax.random.randint(key, (LEAVES, NEAR), -LDEV, LDEV + 1)
    column = jnp.arange(NEAR)[None, :]
    offsets = jnp.where(column == 0, 0, offsets)
    return ((jnp.arange(LEAVES)[:, None] + offsets) % LEAVES).astype(jnp.int32)


def draw_near_count(key, part):
    key = jax.random.fold_in(key, 2)
    first, second = jax.random.split(key)
    highest = jax.random.randint(first, (LEAVES // LDEV,), 2, NEAR + 1)
    spread = jax.random.randint(second, (LEAVES,), 0, 1048576)
    counts = 1 + spread % jnp.repeat(highest, LDEV)
    counts = jnp.where(jnp.arange(LEAVES) == 0, NEAR, counts)
    return counts.astype(jnp.int32)


def draw_far_index(key, part):
    key = jax.random.fold_in(key, 3)
    offsets = jax.random.randint(key, (LEAVES, FARL), -LDEV, LDEV + 1)
    return ((jnp.arange(LEAVES)[:, None] + offsets) % LEAVES).astype(jnp.int32)


def draw_cluster_index(key, part):
    key = jax.random.fold_in(key, 4)
    reach = min(FARC, (CLUSTERS - 1) // 2)
    offsets = jax.random.randint(key, (CLUSTERS, FARC), -reach, reach + 1)
    column = jnp.arange(FARC)[None, :]
    offsets = jnp.where(column == 0, -reach, offsets)
    offsets = jnp.where(column == 1, reach, offsets)
    return ((jnp.arange(CLUSTERS)[:, None] + offsets) % CLUSTERS).astype(jnp.int32)


def shard_levels(key, dims, cuts, least, high):
    factor_of = 1.0
    for axis_at, shards_of in cuts:
        draws = jax.random.uniform(jax.random.fold_in(jax.random.fold_in(key, 6), axis_at), (shards_of,), jnp.float32, least / len(cuts), high / len(cuts))
        factor_of = factor_of * jnp.repeat(jnp.exp(draws), dims[axis_at] // shards_of).reshape((-1,) + (1,) * (len(dims) - 1 - axis_at))
    return factor_of


def bell_draw(own_key, shape, scale, bound, shards=(), dtype=jnp.bfloat16):
    gain = shard_levels(own_key, shape, shards, -0.22, 0.18) if shards else 1.0
    drawn = jax.random.normal(own_key, shape, jnp.float32) * scale * gain
    return jnp.minimum(jnp.maximum(drawn, -bound), bound).astype(dtype)


def setup_inputs(seed: int = 0, part: int = 0) -> dict:
    key_list = jax.random.split(jax.random.key(seed), 11)
    part_splits = jax.random.split(jax.random.fold_in(key_list[10], part), 11)
    charges = bell_draw(part_splits[0], (LEAVES, RHS, LS), 1.0, 6.0, ((0, 16),))
    near_blocks = bell_draw(part_splits[1], (LEAVES, NEAR, LS, LS), (LS * NEAR) ** -0.5, 0.1875, ((0, 16),))
    near_index = draw_near_index(jax.random.fold_in(jax.random.fold_in(key_list[10], part), 71), part)
    near_count = draw_near_count(jax.random.fold_in(jax.random.fold_in(key_list[10], part), 71), part)
    leaf_basis = bell_draw(part_splits[4], (LEAVES, RANK, LS), LS ** -0.5, 0.5, ((0, 16),))
    leaf_coupling = bell_draw(part_splits[5], (LEAVES, FARL, RANK, RANK), (RANK * FARL) ** -0.5, 0.25, ((0, 16),))
    far_index = draw_far_index(jax.random.fold_in(jax.random.fold_in(key_list[10], part), 71), part)
    transfer = bell_draw(part_splits[7], (LEAVES, RANK, RANK), RANK ** -0.5, 0.75, ((0, 16),))
    cluster_coupling = bell_draw(part_splits[8], (CLUSTERS, FARC, RANK, RANK), (RANK * FARC * LDEV) ** -0.5, 0.03125, ((0, 16),))
    cluster_index = draw_cluster_index(jax.random.fold_in(jax.random.fold_in(key_list[10], part), 71), part)
    return {"charges": charges, "near_blocks": near_blocks, "near_index": near_index, "near_count": near_count, "leaf_basis": leaf_basis, "leaf_coupling": leaf_coupling, "far_index": far_index, "transfer": transfer, "cluster_coupling": cluster_coupling, "cluster_index": cluster_index}


def reference(charges, near_blocks, near_index, near_count, leaf_basis, leaf_coupling, far_index, transfer, cluster_coupling, cluster_index):
    high = lax.Precision.HIGHEST
    charges_f = charges.astype(jnp.float32)
    basis_f = leaf_basis.astype(jnp.float32)
    transfer_f = transfer.astype(jnp.float32)
    moments = jnp.einsum('irp,ikp->irk', charges_f, basis_f, precision=high).astype(jnp.bfloat16)
    moments_f = moments.astype(jnp.float32)
    lifted = jnp.einsum('irk,ick->irc', moments_f, transfer_f, precision=high)
    cluster_moments = jnp.sum(lifted.reshape(CLUSTERS, LDEV, RHS, RANK), axis=1)
    cluster_local = jnp.zeros((CLUSTERS, RHS, RANK), jnp.float32)
    for entry in range(FARC):
        picked = cluster_moments[cluster_index[:, entry]]
        cluster_local = cluster_local + jnp.einsum('crk,ctk->crt', picked, cluster_coupling[:, entry].astype(jnp.float32), precision=high)
    leaf_far = jnp.zeros((LEAVES, RHS, RANK), jnp.float32)
    for entry in range(FARL):
        picked = moments_f[far_index[:, entry]]
        leaf_far = leaf_far + jnp.einsum('irk,itk->irt', picked, leaf_coupling[:, entry].astype(jnp.float32), precision=high)
    spread = jnp.repeat(cluster_local, LDEV, axis=0)
    leaf_local = (leaf_far + jnp.einsum('irc,ick->irk', spread, transfer_f, precision=high)).astype(jnp.bfloat16)
    near_sum = jnp.zeros((LEAVES, RHS, LS), jnp.float32)
    for slot in range(NEAR):
        picked = charges_f[near_index[:, slot]]
        term = jnp.einsum('irp,itp->irt', picked, near_blocks[:, slot].astype(jnp.float32), precision=high)
        near_sum = near_sum + jnp.where((slot < near_count)[:, None, None], term, 0.0)
    far_part = jnp.einsum('irk,ikp->irp', leaf_local.astype(jnp.float32), basis_f, precision=high)
    return (far_part + near_sum).astype(jnp.bfloat16)
```

```python
import functools

import jax
import jax.numpy as jnp
from jax import lax
from jax.experimental import pallas as pl
from jax.experimental.pallas import tpu as pltpu
from jax.sharding import PartitionSpec as P

MESH = pl.DeviceIdType.MESH
F32 = jnp.float32
BF16 = jnp.bfloat16


def dot_t(a, b):
    return lax.dot_general(a, b, (((1,), (1,)), ((), ())), preferred_element_type=F32)


def kernel(
    n, reach, chunks, size, early,
    ch, nb, ni, nc, lb, lc, fi, tr, cc, ci, out,
    cst, mst, hslow_c, hslow_m, hfast_m, mpack, tpk, basis, trans, ccv, cmall, cmown, nbuf, cbuf, obuf,
    fc_send, fc_recv, fm_send, fm_recv, sc_send, sc_recv, sm_send, sm_recv, cl_send, cl_recv,
    own_sem, near_sem, coup_sem, out_sem,
):
    leaves = chunks * size
    total = n * leaves
    slots = ni.shape[0]
    farl = fi.shape[0]
    me = lax.axis_index("leaf")
    odd = lax.rem(me, 2)
    even = 1 - odd
    first = me * leaves
    fast = me + 1 - 2 * odd
    slow = lax.rem(me - 1 + 2 * odd + n, n)

    def block(q):
        return q + even * (chunks - 1 - 2 * q)

    def sent(q):
        return q + odd * (chunks - 1 - 2 * q)

    own = [
        pltpu.make_async_copy(ch, cst.at[pl.ds(leaves, leaves)], own_sem.at[0]),
        pltpu.make_async_copy(lb, basis, own_sem.at[1]),
        pltpu.make_async_copy(tr, trans, own_sem.at[2]),
        pltpu.make_async_copy(cc, ccv, own_sem.at[3]),
    ]
    for copy in own:
        copy.start()

    barrier = pltpu.get_barrier_semaphore()
    for o in range(1, reach + 1):
        for d in (o, n - o):
            pl.semaphore_signal(
                barrier, inc=1, device_id={"leaf": lax.rem(me + d, n)}, device_id_type=MESH
            )
    pl.semaphore_wait(barrier, 2 * reach)

    def remote(src, dst, send, recv, d):
        return pltpu.make_async_remote_copy(
            src_ref=src, dst_ref=dst, send_sem=send, recv_sem=recv,
            device_id={"leaf": d}, device_id_type=MESH,
        )

    def slow_c(q):
        return remote(
            ch.at[pl.ds(sent(q) * size, size)], hslow_c.at[q], sc_send.at[q], sc_recv.at[q], slow
        )

    def slow_m(q):
        return remote(mpack.at[sent(q)], hslow_m.at[q], sm_send.at[q], sm_recv.at[q], slow)

    fast_c = remote(
        ch, cst.at[pl.ds(odd * (2 * leaves), leaves)], fc_send.at[0], fc_recv.at[0], fast
    )
    fast_m = remote(mpack, hfast_m, fm_send.at[0], fm_recv.at[0], fast)

    def near_copy(q):
        return pltpu.make_async_copy(
            nb.at[pl.ds(block(q) * size, size)], nbuf.at[q], near_sem.at[q]
        )

    def coup_copy(q):
        return pltpu.make_async_copy(
            lc.at[pl.ds(block(q) * size, size)], cbuf.at[q], coup_sem.at[q]
        )

    def out_copy(q):
        return pltpu.make_async_copy(
            obuf.at[q], out.at[pl.ds(block(q) * size, size)], out_sem.at[q]
        )

    def loop(lo, hi, body):
        def step(i, c):
            body(i)
            return c
        lax.fori_loop(lo, hi, step, 0)

    loop(0, early, lambda q: slow_c(q).start())
    fast_c.start()
    cst[3 * leaves] = jnp.zeros(cst.shape[1:], BF16)
    for copy in own[:3]:
        copy.wait()

    left = lax.broadcasted_iota(jnp.int32, (ch.shape[1], 128), 1) < 64

    def lift_step(b, lift):
        for j in range(size // 2):
            both = []
            for h in range(2):
                leaf = b * size + 2 * j + h
                twice = jnp.concatenate([basis[leaf], basis[leaf]], axis=0)
                m = dot_t(cst[leaves + leaf], twice)
                mst[leaves + leaf] = m.astype(BF16)
                both.append(m)
            packed = jnp.where(left, both[0], both[1]).astype(BF16)
            mpack[b, j] = packed
            pair = jnp.concatenate(
                [trans[b * size + 2 * j], trans[b * size + 2 * j + 1]], axis=1
            )
            tpk[b, j] = pair
            lift = lift + dot_t(packed, pair)
        return lift

    rank = lb.shape[1]
    lift = lax.fori_loop(0, chunks, lift_step, jnp.zeros((ch.shape[1], rank), F32))
    half = lift.shape[0] // 2
    lifted = jnp.concatenate([lift[:half], lift[half:]], axis=1).astype(BF16)
    cmown[...] = lifted
    cmall[reach] = lifted

    def cluster(o):
        at = 0 if o < 0 else 1
        i = 2 * (abs(o) - 1) + at
        j = 2 * (abs(o) - 1) + at
        return remote(
            cmown, cmall.at[reach - o], cl_send.at[i], cl_recv.at[j], lax.rem(me + o + n, n)
        )

    offsets = [s * o for o in range(reach, 0, -1) for s in (1, -1)]
    for o in offsets:
        cluster(o).start()
    fast_m.start()

    def rest(q):
        slow_m(q).start()
        slow_c(q + early).start()

    loop(0, chunks - early, rest)
    loop(chunks - early, chunks, lambda q: slow_m(q).start())

    def fetch(q):
        near_copy(q).start()
        coup_copy(q).start()

    loop(0, chunks, fetch)

    def spread(packed, at):
        a = packed[:, :64]
        b = packed[:, 64:]
        mst[at] = jnp.concatenate([a, a], axis=1)
        mst[at + 1] = jnp.concatenate([b, b], axis=1)

    fast_c.wait_recv()
    fast_m.wait_recv()
    fast_base = even * (2 * leaves)
    slow_base = odd * (2 * leaves)

    def unpack_fast(b):
        for j in range(size // 2):
            spread(hfast_m[b, j], fast_base + b * size + 2 * j)

    loop(0, chunks, unpack_fast)

    own[3].wait()
    for o in offsets:
        cluster(o).wait_recv()
    local = jnp.zeros((ch.shape[1], rank), F32)
    for f in range(ci.shape[1]):
        slot = jnp.clip(lax.rem(ci[0, f] - me + reach + n, n), 0, 2 * reach)
        p = cmall[slot]
        picked = jnp.concatenate([p[:, :64], p[:, 64:]], axis=0)
        local = local + dot_t(picked, ccv[0, f])
    local = local.astype(BF16)

    def work(q):
        slow_c(q).wait_recv()
        slow_m(q).wait_recv()
        near_copy(q).wait()
        coup_copy(q).wait()
        b = block(q)
        cst[pl.ds(slow_base + b * size, size)] = hslow_c[q]
        for j in range(size // 2):
            spread(hslow_m[q, j], slow_base + b * size + 2 * j)

        def place(index):
            return jnp.clip(lax.rem(index - first + leaves + total, total), 0, 3 * leaves - 1)

        for j in range(size // 2):
            down = jnp.dot(local, tpk[b, j], preferred_element_type=F32)
            for h in range(2):
                at = 2 * j + h
                leaf = b * size + at
                count = nc[leaf]
                lhs, rhs = [], []
                for s in range(slots):
                    pos = jnp.where(s < count, place(ni[s, leaf]), 3 * leaves)
                    lhs.append(cst[pos])
                    rhs.append(nbuf[q, at, s])
                near = dot_t(jnp.concatenate(lhs, axis=1), jnp.concatenate(rhs, axis=1))
                lhs, rhs = [], []
                for f in range(0, farl, 2):
                    lhs.append(
                        jnp.where(left, mst[place(fi[f, leaf])], mst[place(fi[f + 1, leaf])])
                    )
                    rhs.append(
                        jnp.concatenate([cbuf[q, at, f], cbuf[q, at, f + 1]], axis=1)
                    )
                far = dot_t(jnp.concatenate(lhs, axis=1), jnp.concatenate(rhs, axis=1))
                ll = (far + down[:, h * 64 : h * 64 + 64]).astype(BF16)
                far_part = jnp.dot(ll, basis[leaf], preferred_element_type=F32)
                obuf[q, at] = (near + far_part).astype(BF16)
        out_copy(q).start()

    loop(0, chunks, work)

    def finish(q):
        out_copy(q).wait()
        slow_c(q).wait_send()
        slow_m(q).wait_send()

    loop(0, chunks, finish)
    fast_c.wait_send()
    fast_m.wait_send()
    for o in offsets:
        cluster(o).wait_send()


def shards(n, charges, near_blocks, near_index, near_count, leaf_basis, leaf_coupling,
           far_index, transfer, cluster_coupling, cluster_index):
    leaves, rhs, points = charges.shape
    rank = leaf_basis.shape[1]
    size = 4
    chunks = leaves // size
    early = 2
    reach = min(16, (n - 1) // 2)
    hbm = pl.BlockSpec(memory_space=pl.ANY)
    smem = pl.BlockSpec(memory_space=pltpu.SMEM)
    dma = pltpu.SemaphoreType.DMA
    packed = (chunks, size // 2, rhs, 2 * rank)
    return pl.pallas_call(
        functools.partial(kernel, n, reach, chunks, size, early),
        out_shape=jax.ShapeDtypeStruct(charges.shape, BF16),
        in_specs=[hbm, hbm, smem, smem, hbm, hbm, smem, hbm, hbm, smem],
        out_specs=hbm,
        scratch_shapes=[
            pltpu.VMEM((3 * leaves + 1, rhs, points), BF16),
            pltpu.VMEM((3 * leaves, rhs, 2 * rank), BF16),
            pltpu.VMEM((chunks, size, rhs, points), BF16),
            pltpu.VMEM(packed, BF16),
            pltpu.VMEM(packed, BF16),
            pltpu.VMEM(packed, BF16),
            pltpu.VMEM((chunks, size // 2, rank, 2 * rank), BF16),
            pltpu.VMEM(leaf_basis.shape, BF16),
            pltpu.VMEM(transfer.shape, BF16),
            pltpu.VMEM(cluster_coupling.shape, BF16),
            pltpu.VMEM((2 * reach + 1, rhs // 2, 2 * rank), BF16),
            pltpu.VMEM((rhs // 2, 2 * rank), BF16),
            pltpu.VMEM((chunks, size) + near_blocks.shape[1:], BF16),
            pltpu.VMEM((chunks, size) + leaf_coupling.shape[1:], BF16),
            pltpu.VMEM((chunks, size, rhs, points), BF16),
            dma((1,)), dma((1,)), dma((1,)), dma((1,)),
            dma((chunks,)), dma((chunks,)), dma((chunks,)), dma((chunks,)),
            dma((2 * reach,)), dma((2 * reach,)),
            dma((4,)), dma((chunks,)), dma((chunks,)), dma((chunks,)),
        ],
        compiler_params=pltpu.CompilerParams(
            collective_id=0, has_side_effects=True, vmem_limit_bytes=60 * 1024 * 1024
        ),
    )(charges, near_blocks, near_index.T, near_count, leaf_basis, leaf_coupling,
      far_index.T, transfer, cluster_coupling, cluster_index)


def solution(mesh):
    three = P(("parts", "leaf"), None, None)
    four = P(("parts", "leaf"), None, None, None)
    two = P(("parts", "leaf"), None)
    placed = (three, four, two, P(("parts", "leaf")), three, four, two, three, four, two)
    return jax.shard_map(
        functools.partial(shards, mesh.shape["leaf"]),
        mesh=mesh,
        in_specs=placed,
        out_specs=three,
        check_vma=False,
    )
```

```python
import functools

import jax
import jax.numpy as jnp
from jax import lax
from jax.experimental import pallas as pl
from jax.experimental.pallas import tpu as pltpu
from jax.sharding import PartitionSpec as P

MESH = pl.DeviceIdType.MESH
F32 = jnp.float32
BF16 = jnp.bfloat16


def dot_t(a, b):
    return lax.dot_general(a, b, (((1,), (1,)), ((), ())), preferred_element_type=F32)


def kernel(
    n, chunks, size, early, parted,
    ch, nb, ni, nc, lb, lc, fi, tr, cc, ci, out,
    cst, mst, hslow_c, hslow_m, hfast_m, mpack, tpk, basis, trans, ccv, cmall, nbuf, cbuf, nsum, fsum,
    fc_send, fc_recv, fm_send, fm_recv, sc_send, sc_recv, sm_send, sm_recv, cl_send, cl_recv,
    own_sem, near_sem, coup_sem,
):
    leaves = chunks * size
    total = n * leaves
    slots = ni.shape[0]
    farl = fi.shape[0]
    me = lax.axis_index("leaf")
    odd = lax.rem(me, 2)
    even = 1 - odd
    first = me * leaves
    fast = me + 1 - 2 * odd
    slow = lax.rem(me - 1 + 2 * odd + n, n)

    def block(q):
        return q + even * (chunks - 1 - 2 * q)

    def sent(q):
        return q + odd * (chunks - 1 - 2 * q)

    reach = min(16, (n - 1) // 2)
    offsets = [t * o for o in range(reach, 0, -1) for t in (1, -1)]
    barrier = pltpu.get_barrier_semaphore()
    for o in offsets:
        d = lax.rem(me + o + n, n)
        pl.semaphore_signal(barrier, inc=1, device_id={"leaf": d}, device_id_type=MESH)

    own = [
        pltpu.make_async_copy(ch, cst.at[pl.ds(leaves, leaves)], own_sem.at[0]),
        pltpu.make_async_copy(lb, basis, own_sem.at[1]),
        pltpu.make_async_copy(tr, trans, own_sem.at[2]),
        pltpu.make_async_copy(cc, ccv, own_sem.at[3]),
    ]
    for copy in own:
        copy.start()

    def near_copy(q):
        return pltpu.make_async_copy(
            nb.at[pl.ds(block(q) * size, size)], nbuf.at[q], near_sem.at[q]
        )

    def coup_copy(q):
        return pltpu.make_async_copy(
            lc.at[pl.ds(block(q) * size, size)], cbuf.at[q], coup_sem.at[q]
        )

    def loop(lo, hi, body):
        def step(i, c):
            body(i)
            return c
        lax.fori_loop(lo, hi, step, 0)

    def fetch(q):
        near_copy(q).start()
        coup_copy(q).start()

    loop(0, chunks, fetch)
    pl.semaphore_wait(barrier, len(offsets))

    def remote(src, dst, send, recv, d):
        return pltpu.make_async_remote_copy(
            src_ref=src, dst_ref=dst, send_sem=send, recv_sem=recv,
            device_id={"leaf": d}, device_id_type=MESH,
        )

    def slow_c(q):
        return remote(
            ch.at[pl.ds(sent(q) * size, size)], hslow_c.at[q], sc_send.at[q], sc_recv.at[q], slow
        )

    def slow_m(q):
        return remote(mpack.at[sent(q)], hslow_m.at[q], sm_send.at[q], sm_recv.at[q], slow)

    fast_c = remote(
        ch, cst.at[pl.ds(odd * (2 * leaves), leaves)], fc_send.at[0], fc_recv.at[0], fast
    )
    fast_m = remote(mpack, hfast_m, fm_send.at[0], fm_recv.at[0], fast)

    loop(0, early, lambda q: slow_c(q).start())
    fast_c.start()
    cst[3 * leaves] = jnp.zeros(cst.shape[1:], BF16)
    for copy in own[:3]:
        copy.wait()

    left = lax.broadcasted_iota(jnp.int32, (ch.shape[1], 128), 1) < 64

    wide = 2

    def lift_step(g, lift):
        packs, pairs = [], []
        for i in range(wide * size // 2):
            leaf = g * (wide * size) + 2 * i
            b, j = g * wide + i // (size // 2), i % (size // 2)
            both = []
            for h in range(2):
                twice = jnp.concatenate([basis[leaf + h], basis[leaf + h]], axis=0)
                m = dot_t(cst[leaves + leaf + h], twice)
                mst[leaves + leaf + h] = m.astype(BF16)
                both.append(m)
            packed = jnp.where(left, both[0], both[1]).astype(BF16)
            mpack[b, j] = packed
            pair = jnp.concatenate([trans[leaf], trans[leaf + 1]], axis=1)
            tpk[b, j] = pair
            packs.append(packed)
            pairs.append(pair)
        return lift + dot_t(jnp.concatenate(packs, axis=1), jnp.concatenate(pairs, axis=1))

    def two_parts(x):
        high = x.astype(BF16)
        low = (x - high.astype(F32)).astype(BF16)
        return jnp.concatenate([high, low], axis=1)

    def folded(x):
        half = x.shape[0] // 2
        return jnp.concatenate([x[:half], x[half:]], axis=1).astype(BF16)

    def unfolded(p):
        return jnp.concatenate([p[:, :rank], p[:, rank:]], axis=0)

    rank = lb.shape[1]
    lift = lax.fori_loop(0, chunks // wide, lift_step, jnp.zeros((ch.shape[1], rank), F32))
    cmall[me] = folded(lift)
    spots = [
        remote(cmall.at[me], cmall.at[me], cl_send.at[k], cl_recv.at[k], lax.rem(me + o + n, n))
        for k, o in enumerate(offsets)
    ]
    for copy in spots:
        copy.start()
    fast_m.start()
    loop(0, 1, lambda q: slow_m(q).start())

    def spread(packed, at):
        a = packed[:, :64]
        b = packed[:, 64:]
        mst[at] = jnp.concatenate([a, a], axis=1)
        mst[at + 1] = jnp.concatenate([b, b], axis=1)

    loop(1, 2, lambda q: slow_m(q).start())
    loop(early, early + 1, lambda q: slow_c(q).start())
    fast_c.wait_recv()
    fast_m.wait_recv()
    fast_base = even * (2 * leaves)
    slow_base = odd * (2 * leaves)

    def unpack_fast(b):
        for j in range(size // 2):
            spread(hfast_m[b, j], fast_base + b * size + 2 * j)

    loop(0, chunks, unpack_fast)

    own[3].wait()

    def push(q):
        slow_m(q + 2).start()
        slow_c(q + early + 1).start()

    tail = chunks - early - 1
    loop(0, tail, push)
    loop(tail + 2, chunks, lambda q: slow_m(q).start())

    def lowered(local, b, j):
        twice = jnp.concatenate([tpk[b, j], tpk[b, j]], axis=0)
        return jnp.dot(local, twice, preferred_element_type=F32)

    def close(leaf, near, far, down):
        ll = (far + down).astype(BF16)
        far_part = jnp.dot(ll, basis[leaf], preferred_element_type=F32)
        out[leaf] = (near + far_part).astype(BF16)

    def work(q, local=None):
        slow_c(q).wait_recv()
        slow_m(q).wait_recv()
        near_copy(q).wait()
        coup_copy(q).wait()
        b = block(q)
        cst[pl.ds(slow_base + b * size, size)] = hslow_c[q]
        for j in range(size // 2):
            spread(hslow_m[q, j], slow_base + b * size + 2 * j)

        def place(index):
            return jnp.clip(lax.rem(index - first + leaves + total, total), 0, 3 * leaves - 1)

        for j in range(size // 2):
            if local is not None:
                down = lowered(local, b, j)
            for h in range(2):
                at = 2 * j + h
                leaf = b * size + at
                count = nc[leaf]
                lhs, rhs = [], []
                for s in range(slots):
                    pos = jnp.where(s < count, place(ni[s, leaf]), 3 * leaves)
                    lhs.append(cst[pos])
                    rhs.append(nbuf[q, at, s])
                near = dot_t(jnp.concatenate(lhs, axis=1), jnp.concatenate(rhs, axis=1))
                lhs, rhs = [], []
                for f in range(0, farl, 2):
                    lhs.append(
                        jnp.where(left, mst[place(fi[f, leaf])], mst[place(fi[f + 1, leaf])])
                    )
                    rhs.append(
                        jnp.concatenate([cbuf[q, at, f], cbuf[q, at, f + 1]], axis=1)
                    )
                far = dot_t(jnp.concatenate(lhs, axis=1), jnp.concatenate(rhs, axis=1))
                if local is None:
                    nsum[leaf] = near
                    fsum[leaf] = far
                else:
                    close(leaf, near, far, down[:, h * rank : h * rank + rank])

    loop(0, parted, work)
    rhs = [ccv[0, f] for f in range(ci.shape[1])]
    for k, o in enumerate(offsets):
        source = lax.rem(me - o + n, n)
        remote(
            cmall.at[source], cmall.at[source], cl_send.at[k], cl_recv.at[k], fast
        ).wait_recv()
    lhs = []
    for f in range(ci.shape[1]):
        source = jnp.clip(ci[0, f], 0, n - 1)
        lhs.append(unfolded(cmall[source]))
    local = two_parts(dot_t(jnp.concatenate(lhs, axis=1), jnp.concatenate(rhs, axis=1)))

    def settle(q):
        b = block(q)
        for j in range(size // 2):
            down = lowered(local, b, j)
            for h in range(2):
                leaf = b * size + 2 * j + h
                close(leaf, nsum[leaf], fsum[leaf], down[:, h * rank : h * rank + rank])

    loop(0, parted, settle)
    loop(parted, chunks, lambda q: work(q, local))

    def finish(q):
        slow_c(q).wait_send()
        slow_m(q).wait_send()

    loop(0, chunks, finish)
    fast_c.wait_send()
    fast_m.wait_send()
    for copy in spots:
        copy.wait_send()


def shards(n, charges, near_blocks, near_index, near_count, leaf_basis, leaf_coupling,
           far_index, transfer, cluster_coupling, cluster_index):
    leaves, rhs, points = charges.shape
    rank = leaf_basis.shape[1]
    size = 4
    chunks = leaves // size
    early = 2
    reach = min(16, (n - 1) // 2)
    hbm = pl.BlockSpec(memory_space=pl.ANY)
    smem = pl.BlockSpec(memory_space=pltpu.SMEM)
    dma = pltpu.SemaphoreType.DMA
    packed = (chunks, size // 2, rhs, 2 * rank)
    return pl.pallas_call(
        functools.partial(kernel, n, chunks, size, early, 0),
        out_shape=pltpu.VMEM(charges.shape, BF16),
        in_specs=[hbm, hbm, smem, smem, hbm, hbm, smem, hbm, hbm, smem],
        out_specs=pl.BlockSpec(memory_space=pltpu.VMEM),
        scratch_shapes=[
            pltpu.VMEM((3 * leaves + 1, rhs, points), BF16),
            pltpu.VMEM((3 * leaves, rhs, 2 * rank), BF16),
            pltpu.VMEM((chunks, size, rhs, points), BF16),
            pltpu.VMEM(packed, BF16),
            pltpu.VMEM(packed, BF16),
            pltpu.VMEM(packed, BF16),
            pltpu.VMEM((chunks, size // 2, rank, 2 * rank), BF16),
            pltpu.VMEM(leaf_basis.shape, BF16),
            pltpu.VMEM(transfer.shape, BF16),
            pltpu.VMEM(cluster_coupling.shape, BF16),
            pltpu.VMEM((n, rhs // 2, 2 * rank), BF16),
            pltpu.VMEM((chunks, size) + near_blocks.shape[1:], BF16),
            pltpu.VMEM((chunks, size) + leaf_coupling.shape[1:], BF16),
            pltpu.VMEM(charges.shape, F32),
            pltpu.VMEM((leaves, rhs, rank), F32),
            dma((1,)), dma((1,)), dma((1,)), dma((1,)),
            dma((chunks,)), dma((chunks,)), dma((chunks,)), dma((chunks,)),
            dma((2 * reach,)), dma((2 * reach,)),
            dma((4,)), dma((chunks,)), dma((chunks,)),
        ],
        compiler_params=pltpu.CompilerParams(
            collective_id=0, has_side_effects=True, vmem_limit_bytes=60 * 1024 * 1024
        ),
    )(charges, near_blocks, near_index.T, near_count, leaf_basis, leaf_coupling,
      far_index.T, transfer, cluster_coupling, cluster_index)


def solution(mesh):
    three = P(("parts", "leaf"), None, None)
    four = P(("parts", "leaf"), None, None, None)
    two = P(("parts", "leaf"), None)
    placed = (three, four, two, P(("parts", "leaf")), three, four, two, three, four, two)
    return jax.shard_map(
        functools.partial(shards, mesh.shape["leaf"]),
        mesh=mesh,
        in_specs=placed,
        out_specs=three,
        check_vma=False,
    )
```

```python
import functools

import jax
import jax.numpy as jnp
from jax import lax
from jax.experimental import pallas as pl
from jax.experimental.pallas import tpu as pltpu
from jax.sharding import PartitionSpec as P

MESH = pl.DeviceIdType.MESH
F32 = jnp.float32
BF16 = jnp.bfloat16


def dot_t(a, b):
    return lax.dot_general(a, b, (((1,), (1,)), ((), ())), preferred_element_type=F32)


def kernel(
    n, chunks, size, early, parted,
    ch, nb, ni, nc, lb, lc, fi, tr, cc, ci, out,
    cst, mst, hslow_c, hslow_m, hfast_m, mpack, tpk, basis, trans, ccv, cmall, nbuf, cbuf, nsum, fsum,
    fc_send, fc_recv, fm_send, fm_recv, sc_send, sc_recv, sm_send, sm_recv, cl_send, cl_recv,
    own_sem, near_sem, coup_sem,
):
    leaves = chunks * size
    total = n * leaves
    slots = ni.shape[0]
    farl = fi.shape[0]
    me = lax.axis_index("leaf")
    odd = lax.rem(me, 2)
    even = 1 - odd
    first = me * leaves
    fast = me + 1 - 2 * odd
    slow = lax.rem(me - 1 + 2 * odd + n, n)

    def block(q):
        return q + even * (chunks - 1 - 2 * q)

    def sent(q):
        return q + odd * (chunks - 1 - 2 * q)

    reach = min(16, (n - 1) // 2)
    offsets = [t * o for o in range(reach, 0, -1) for t in (1, -1)]
    barrier = pltpu.get_barrier_semaphore()
    for o in offsets:
        d = lax.rem(me + o + n, n)
        pl.semaphore_signal(barrier, inc=1, device_id={"leaf": d}, device_id_type=MESH)

    own = [
        pltpu.make_async_copy(ch, cst.at[pl.ds(leaves, leaves)], own_sem.at[0]),
        pltpu.make_async_copy(lb, basis, own_sem.at[1]),
        pltpu.make_async_copy(tr, trans, own_sem.at[2]),
        pltpu.make_async_copy(cc, ccv, own_sem.at[3]),
    ]
    for copy in own:
        copy.start()

    def near_copy(q):
        return pltpu.make_async_copy(
            nb.at[pl.ds(block(q) * size, size)], nbuf.at[q], near_sem.at[q]
        )

    def coup_copy(q):
        return pltpu.make_async_copy(
            lc.at[pl.ds(block(q) * size, size)], cbuf.at[q], coup_sem.at[q]
        )

    def loop(lo, hi, body):
        def step(i, c):
            body(i)
            return c
        lax.fori_loop(lo, hi, step, 0)

    def fetch(q):
        near_copy(q).start()
        coup_copy(q).start()

    loop(0, chunks, fetch)
    pl.semaphore_wait(barrier, len(offsets))

    def remote(src, dst, send, recv, d):
        return pltpu.make_async_remote_copy(
            src_ref=src, dst_ref=dst, send_sem=send, recv_sem=recv,
            device_id={"leaf": d}, device_id_type=MESH,
        )

    def slow_c(q):
        return remote(
            ch.at[pl.ds(sent(q) * size, size)], hslow_c.at[q], sc_send.at[q], sc_recv.at[q], slow
        )

    def slow_m(q):
        return remote(mpack.at[sent(q)], hslow_m.at[q], sm_send.at[q], sm_recv.at[q], slow)

    fast_c = remote(
        ch, cst.at[pl.ds(odd * (2 * leaves), leaves)], fc_send.at[0], fc_recv.at[0], fast
    )
    fast_m = remote(mpack, hfast_m, fm_send.at[0], fm_recv.at[0], fast)

    loop(0, early, lambda q: slow_c(q).start())
    fast_c.start()
    cst[3 * leaves] = jnp.zeros(cst.shape[1:], BF16)
    for copy in own[:3]:
        copy.wait()

    left = lax.broadcasted_iota(jnp.int32, (ch.shape[1], 128), 1) < 64

    wide = 4

    def lift_step(g, lift):
        packs, pairs = [], []
        for i in range(wide * size // 2):
            leaf = g * (wide * size) + 2 * i
            b, j = g * wide + i // (size // 2), i % (size // 2)
            both = []
            for h in range(2):
                twice = jnp.concatenate([basis[leaf + h], basis[leaf + h]], axis=0)
                m = dot_t(cst[leaves + leaf + h], twice)
                mst[leaves + leaf + h] = m.astype(BF16)
                both.append(m)
            packed = jnp.where(left, both[0], both[1]).astype(BF16)
            mpack[b, j] = packed
            pair = jnp.concatenate([trans[leaf], trans[leaf + 1]], axis=1)
            tpk[b, j] = pair
            packs.append(packed)
            pairs.append(pair)
        return lift + dot_t(jnp.concatenate(packs, axis=1), jnp.concatenate(pairs, axis=1))

    def two_parts(x):
        high = x.astype(BF16)
        low = (x - high.astype(F32)).astype(BF16)
        return jnp.concatenate([high, low], axis=1)

    def folded(x):
        half = x.shape[0] // 2
        return jnp.concatenate([x[:half], x[half:]], axis=1).astype(BF16)

    def unfolded(p):
        return jnp.concatenate([p[:, :rank], p[:, rank:]], axis=0)

    rank = lb.shape[1]
    lift = lax.fori_loop(0, chunks // wide, lift_step, jnp.zeros((ch.shape[1], rank), F32))
    cmall[me] = folded(lift)
    spots = [
        remote(cmall.at[me], cmall.at[me], cl_send.at[k], cl_recv.at[k], lax.rem(me + o + n, n))
        for k, o in enumerate(offsets)
    ]
    for copy in spots:
        copy.start()
    fast_m.start()
    loop(0, 1, lambda q: slow_m(q).start())

    def spread(packed, at):
        a = packed[:, :64]
        b = packed[:, 64:]
        mst[at] = jnp.concatenate([a, a], axis=1)
        mst[at + 1] = jnp.concatenate([b, b], axis=1)

    loop(1, 2, lambda q: slow_m(q).start())
    loop(early, early + 1, lambda q: slow_c(q).start())
    fast_c.wait_recv()
    fast_m.wait_recv()
    fast_base = even * (2 * leaves)
    slow_base = odd * (2 * leaves)

    def unpack_fast(b):
        for j in range(size // 2):
            spread(hfast_m[b, j], fast_base + b * size + 2 * j)

    loop(0, chunks, unpack_fast)

    own[3].wait()

    def push(q):
        slow_m(q + 2).start()
        slow_c(q + early + 1).start()

    tail = chunks - early - 1
    loop(0, tail, push)
    loop(tail + 2, chunks, lambda q: slow_m(q).start())

    def lowered(local, b, j):
        twice = jnp.concatenate([tpk[b, j], tpk[b, j]], axis=0)
        return jnp.dot(local, twice, preferred_element_type=F32)

    def close(leaf, near, far, down):
        ll = (far + down).astype(BF16)
        far_part = jnp.dot(ll, basis[leaf], preferred_element_type=F32)
        out[leaf] = (near + far_part).astype(BF16)

    def work(q, local=None):
        slow_c(q).wait_recv()
        slow_m(q).wait_recv()
        near_copy(q).wait()
        coup_copy(q).wait()
        b = block(q)
        cst[pl.ds(slow_base + b * size, size)] = hslow_c[q]
        for j in range(size // 2):
            spread(hslow_m[q, j], slow_base + b * size + 2 * j)

        def place(index):
            return jnp.clip(lax.rem(index - first + leaves + total, total), 0, 3 * leaves - 1)

        for j in range(size // 2):
            if local is not None:
                down = lowered(local, b, j)
            for h in range(2):
                at = 2 * j + h
                leaf = b * size + at
                count = nc[leaf]
                lhs, rhs = [], []
                for s in range(slots):
                    pos = jnp.where(s < count, place(ni[s, leaf]), 3 * leaves)
                    lhs.append(cst[pos])
                    rhs.append(nbuf[q, at, s])
                near = dot_t(jnp.concatenate(lhs, axis=1), jnp.concatenate(rhs, axis=1))
                lhs, rhs = [], []
                for f in range(0, farl, 2):
                    lhs.append(
                        jnp.where(left, mst[place(fi[f, leaf])], mst[place(fi[f + 1, leaf])])
                    )
                    rhs.append(
                        jnp.concatenate([cbuf[q, at, f], cbuf[q, at, f + 1]], axis=1)
                    )
                far = dot_t(jnp.concatenate(lhs, axis=1), jnp.concatenate(rhs, axis=1))
                if local is None:
                    nsum[leaf] = near
                    fsum[leaf] = far
                else:
                    close(leaf, near, far, down[:, h * rank : h * rank + rank])

    loop(0, parted, work)
    rhs = [ccv[0, f] for f in range(ci.shape[1])]
    for k, o in enumerate(offsets):
        source = lax.rem(me - o + n, n)
        remote(
            cmall.at[source], cmall.at[source], cl_send.at[k], cl_recv.at[k], fast
        ).wait_recv()
    lhs = []
    for f in range(ci.shape[1]):
        source = jnp.clip(ci[0, f], 0, n - 1)
        lhs.append(unfolded(cmall[source]))
    local = two_parts(dot_t(jnp.concatenate(lhs, axis=1), jnp.concatenate(rhs, axis=1)))

    def settle(q):
        b = block(q)
        for j in range(size // 2):
            down = lowered(local, b, j)
            for h in range(2):
                leaf = b * size + 2 * j + h
                close(leaf, nsum[leaf], fsum[leaf], down[:, h * rank : h * rank + rank])

    loop(0, parted, settle)
    loop(parted, chunks, lambda q: work(q, local))

    def finish(q):
        slow_c(q).wait_send()
        slow_m(q).wait_send()

    loop(0, chunks, finish)
    fast_c.wait_send()
    fast_m.wait_send()
    for copy in spots:
        copy.wait_send()


def shards(n, charges, near_blocks, near_index, near_count, leaf_basis, leaf_coupling,
           far_index, transfer, cluster_coupling, cluster_index):
    leaves, rhs, points = charges.shape
    rank = leaf_basis.shape[1]
    size = 4
    chunks = leaves // size
    early = 1
    reach = min(16, (n - 1) // 2)
    hbm = pl.BlockSpec(memory_space=pl.ANY)
    smem = pl.BlockSpec(memory_space=pltpu.SMEM)
    dma = pltpu.SemaphoreType.DMA
    packed = (chunks, size // 2, rhs, 2 * rank)
    return pl.pallas_call(
        functools.partial(kernel, n, chunks, size, early, 0),
        out_shape=pltpu.VMEM(charges.shape, BF16),
        in_specs=[hbm, hbm, smem, smem, hbm, hbm, smem, hbm, hbm, smem],
        out_specs=pl.BlockSpec(memory_space=pltpu.VMEM),
        scratch_shapes=[
            pltpu.VMEM((3 * leaves + 1, rhs, points), BF16),
            pltpu.VMEM((3 * leaves, rhs, 2 * rank), BF16),
            pltpu.VMEM((chunks, size, rhs, points), BF16),
            pltpu.VMEM(packed, BF16),
            pltpu.VMEM(packed, BF16),
            pltpu.VMEM(packed, BF16),
            pltpu.VMEM((chunks, size // 2, rank, 2 * rank), BF16),
            pltpu.VMEM(leaf_basis.shape, BF16),
            pltpu.VMEM(transfer.shape, BF16),
            pltpu.VMEM(cluster_coupling.shape, BF16),
            pltpu.VMEM((n, rhs // 2, 2 * rank), BF16),
            pltpu.VMEM((chunks, size) + near_blocks.shape[1:], BF16),
            pltpu.VMEM((chunks, size) + leaf_coupling.shape[1:], BF16),
            pltpu.VMEM(charges.shape, F32),
            pltpu.VMEM((leaves, rhs, rank), F32),
            dma((1,)), dma((1,)), dma((1,)), dma((1,)),
            dma((chunks,)), dma((chunks,)), dma((chunks,)), dma((chunks,)),
            dma((2 * reach,)), dma((2 * reach,)),
            dma((4,)), dma((chunks,)), dma((chunks,)),
        ],
        compiler_params=pltpu.CompilerParams(
            collective_id=0, has_side_effects=True, vmem_limit_bytes=60 * 1024 * 1024
        ),
    )(charges, near_blocks, near_index.T, near_count, leaf_basis, leaf_coupling,
      far_index.T, transfer, cluster_coupling, cluster_index)


def solution(mesh):
    three = P(("parts", "leaf"), None, None)
    four = P(("parts", "leaf"), None, None, None)
    two = P(("parts", "leaf"), None)
    placed = (three, four, two, P(("parts", "leaf")), three, four, two, three, four, two)
    return jax.shard_map(
        functools.partial(shards, mesh.shape["leaf"]),
        mesh=mesh,
        in_specs=placed,
        out_specs=three,
        check_vma=False,
    )
```
